512 devices in a mesh: rep: 32 (over y, x, core), seq: 16 (over z).
Axes of the slice: x: 4, y: 4, z: 16, core: 2. Of those that a mesh axis runs over, the one named last changes fastest.
Arguments:
- queries: bfloat16 [8192, 24576], P(('rep', 'seq')), parts along dimension 0, may hold values from -64 to 64
- stretch_latent: bfloat16 [8192, 576], P(('rep', 'seq')), parts along dimension 0, may hold values from -6 to 6
- prefix_latent: bfloat16 [57344, 576], P(('rep', 'seq')), parts along dimension 0, may hold values from -6 to 6
- kv_up_weight: bfloat16 [512, 32768], P(None, 'seq'), may hold values from -0.25 to 0.25
Outputs:
- attended: bfloat16 [8192, 16384], P(('rep', 'seq')), parts along dimension 0
The draws below stay inside these ranges and needn't reach their ends.
There are 32 independent parts, one for each index of `rep`. The reference program is written for one: setup_inputs(seed, part) draws one part's arguments, and reference() takes and returns one part's arrays. A program takes and returns all parts, laid end to end along the dimension named above; an argument that names none is the same for every part. Nothing has to cross between parts.
All inputs are finite; a program needn't handle non-finite values.
Results may differ from the reference program's by a relative error of at most 0.0073.
Values may be sent and summed in bfloat16 or wider, within the bound.
A program may use at most 64 MiB of HBM per device.

```python
import math
import jax
import jax.numpy as jnp
from jax import lax

HEADS = 128
KV_RANK = 512
ROPE = 64
NOPE = 128
VDIM = 128
STRETCH = 256
PREFIX = 1792


def draw_queries(key, part):
    key = jax.random.fold_in(key, 7)
    drawn = 2.5 * jnp.clip(jax.random.normal(key, (STRETCH, HEADS, NOPE + ROPE), jnp.float32), -6.0, 6.0)
    return drawn.reshape(STRETCH, HEADS * (NOPE + ROPE)).astype(jnp.bfloat16)


def draw_prefix_latent(key, part):
    key = jax.random.fold_in(key, 9)
    drawn = jnp.clip(jax.random.normal(key, (PREFIX, KV_RANK + ROPE), jnp.float32), -6.0, 6.0)
    return drawn.astype(jnp.bfloat16)


def level_of(key, extent, shards, smallest, largest):
    level, own = 1.0, jax.random.fold_in(key, 6)
    for axis_at, blocks in shards:
        steps = jnp.exp(jax.random.uniform(jax.random.fold_in(own, axis_at), (blocks,), jnp.float32, smallest / len(shards), largest / len(shards)))
        level = level * jnp.repeat(steps, extent[axis_at] // blocks).reshape([-1 if axis == axis_at else 1 for axis in range(len(extent))])
    return level


def scatter_about(own_key, extent, width, most, pieces=(), kind=jnp.bfloat16):
    entries = jax.random.normal(own_key, extent, jnp.float32) * width
    if len(pieces) > 0:
        entries = level_of(own_key, extent, pieces, -0.22, 0.18) * entries
    return jnp.clip(entries, min=-most, max=most).astype(kind)


def setup_inputs(seed: int = 0, part: int = 0) -> dict:
    keys = jax.random.split(jax.random.key(seed), 5)
    part_keys = jax.random.split(jax.random.fold_in(keys[4], part), 5)
    queries = draw_queries(jax.random.fold_in(jax.random.fold_in(keys[4], part), 71), part)
    stretch_latent = scatter_about(part_keys[1], (STRETCH, KV_RANK + ROPE), 1.0, 6.0, ((0, 16),))
    prefix_latent = draw_prefix_latent(jax.random.fold_in(jax.random.fold_in(keys[4], part), 71), part)
    kv_up_weight = scatter_about(keys[3], (KV_RANK, HEADS * (NOPE + VDIM)), KV_RANK ** -0.5, 0.25, ((1, 16),))
    return dict(queries=queries, stretch_latent=stretch_latent, prefix_latent=prefix_latent, kv_up_weight=kv_up_weight)


def dot_rows(left, right):
    return lax.dot_general(left, right, (((1,), (1,)), ((), ())), preferred_element_type=jnp.float32)

def head_attention(q_head, head_kv, rope_keys, prefix_len):
    score_scale = 1.0 / math.sqrt(NOPE + ROPE)
    q_nope = q_head[:, :NOPE]
    q_rope = q_head[:, NOPE:]
    key_nope = head_kv[:, :NOPE]
    values = head_kv[:, NOPE:]
    scores = (dot_rows(q_nope, key_nope) + dot_rows(q_rope, rope_keys)) * score_scale
    row_index = lax.broadcasted_iota(jnp.int32, scores.shape, 0)
    col_index = lax.broadcasted_iota(jnp.int32, scores.shape, 1)
    visible = col_index <= row_index + prefix_len
    scores = jnp.where(visible, scores, -jnp.inf)
    row_max = lax.optimization_barrier(jnp.max(scores, axis=1, keepdims=True))
    exponent = jnp.where(visible, jnp.exp(scores - row_max), 0.0)
    weights = (exponent / lax.optimization_barrier(jnp.sum(exponent, axis=1, keepdims=True))).astype(jnp.bfloat16)
    return jnp.dot(weights, values, preferred_element_type=jnp.float32).astype(jnp.bfloat16)

def reference(queries, stretch_latent, prefix_latent, kv_up_weight):
    all_latent = jnp.concatenate([prefix_latent, stretch_latent], axis=0)
    rope_keys = all_latent[:, KV_RANK:]
    latent_part = all_latent[:, :KV_RANK]
    query_width = NOPE + ROPE
    head_span = NOPE + VDIM

    def one_head(head_index):
        q_head = lax.dynamic_slice_in_dim(queries, head_index * query_width, query_width, 1)
        weight_cols = lax.dynamic_slice_in_dim(kv_up_weight, head_index * head_span, head_span, 1)
        head_kv = jnp.dot(latent_part, weight_cols, preferred_element_type=jnp.float32).astype(jnp.bfloat16)
        return head_attention(q_head, head_kv, rope_keys, PREFIX)
    per_heads = lax.map(one_head, jnp.arange(HEADS, dtype=jnp.int32))
    return jnp.transpose(per_heads, (1, 0, 2)).reshape(STRETCH, HEADS * VDIM)
```

```python
import functools
import math

import jax
import jax.numpy as jnp
from jax import lax
from jax.experimental import pallas as pl
from jax.experimental.pallas import tpu as pltpu
from jax.sharding import PartitionSpec as P

KV_RANK = 512
ROPE = 64
NOPE = 128
VDIM = 128
QW = NOPE + ROPE
SPAN = NOPE + VDIM
SEQ = 16
HEADS_HERE = 8
PRE = 112
NEW = 16
KEYS = SEQ * (PRE + NEW)
PRE_ALL = SEQ * PRE
WINDOW = 8
ROWS = WINDOW * NEW
CHUNK = 144
SUB = 48
MESH = pl.DeviceIdType.MESH
BF = jnp.bfloat16
F32 = jnp.float32


def mm(a, b):
    return jnp.dot(a, b, preferred_element_type=F32)


def mm_t(a, b):
    return lax.dot_general(a, b, (((1,), (1,)), ((), ())), preferred_element_type=F32)


def kernel(
    reps, prefix, stretch, q_hbm, w_hbm, out_hbm,
    lat, qbuf, wbuf, kbuf, vbuf, ropes, obuf, perm, sel, bias,
    ring_s, ring_r, q_s, q_r, o_s, o_r, w1_s, w1_r, w2_s, w2_r, loc_w, loc_q, loc_o,
):
    me = lax.axis_index("seq")
    rep = lax.axis_index("rep")
    odd = lax.rem(me, 2)
    slice_rows = KV_RANK // reps

    def at(d):
        return lax.rem(me + d + 2 * SEQ, SEQ)

    def first_of(z):
        return -3 - lax.rem(z, 2)

    own_w = pltpu.make_async_copy(w_hbm, wbuf.at[0], loc_w)
    own_w.start()

    lat[me, 0:PRE, :] = prefix[:, 0:KV_RANK]
    lat[me, PRE : PRE + NEW, :] = stretch[:, 0:KV_RANK]
    r64 = lax.broadcasted_iota(jnp.int32, (ROPE, 128), 0)
    c64 = lax.broadcasted_iota(jnp.int32, (ROPE, 128), 1)
    put_low = jnp.where(c64 == r64, 1.0, 0.0).astype(BF)
    put_high = jnp.where(c64 == r64 + ROPE, 1.0, 0.0).astype(BF)
    for t in range(4):
        low = prefix[32 * t : 32 * t + 16, KV_RANK:]
        high = prefix[32 * t + 16 : 32 * t + 32, KV_RANK:] if t < 3 else stretch[:, KV_RANK:]
        lat[me, 128:CHUNK, 128 * t : 128 * t + 128] = (mm(low, put_low) + mm(high, put_high)).astype(BF)

    barrier = pltpu.get_barrier_semaphore()
    z_partners = (1, -1, 2, -2, 3, -3, 4, -4, 8)
    for d in z_partners:
        pl.semaphore_signal(barrier, inc=1, device_id={"seq": at(d)}, device_id_type=MESH)

    def greet(d, c):
        pl.semaphore_signal(barrier, inc=1, device_id={"rep": lax.rem(rep + d, reps)}, device_id_type=MESH)
        return c

    lax.fori_loop(1, reps, greet, 0)
    pl.semaphore_wait(barrier, len(z_partners) + reps - 1)

    my_slice = pl.ds(pl.multiple_of(rep * slice_rows, 16), slice_rows)
    far_w = pltpu.make_async_remote_copy(
        w_hbm.at[my_slice, :], wbuf.at[1, my_slice, :], w1_s, w1_r, device_id={"seq": at(8)}, device_id_type=MESH
    )
    far_w.start()

    def ring(way, step, rows, j):
        held = at(-step) if way == 0 else at(step)
        ref = lat.at[held, rows]
        return pltpu.make_async_remote_copy(
            ref, ref, ring_s.at[way, step, j], ring_r.at[way, step, j],
            device_id={"seq": at(1) if way == 0 else at(-1)}, device_id_type=MESH,
        )

    def ring_in(way, step, rows, j):
        held = at(-step - 1) if way == 0 else at(step + 1)
        ref = lat.at[held, rows]
        return pltpu.make_async_remote_copy(
            ref, ref, ring_s.at[way, step, j], ring_r.at[way, step, j],
            device_id={"seq": at(1) if way == 0 else at(-1)}, device_id_type=MESH,
        )

    subs = [pl.ds(j * SUB, SUB) for j in range(3)]
    halves = [pl.ds(0, 80), pl.ds(80, 64)]
    for j in range(3):
        for way in (0, 1):
            ring(way, 0, subs[j], j).start()

    def q_copy(shard, d):
        z = at(d)
        head_shard = lax.rem(z + 8 * shard, SEQ)
        slot = -d - first_of(z)
        return pltpu.make_async_remote_copy(
            q_hbm.at[:, pl.ds(pl.multiple_of(head_shard * (HEADS_HERE * QW), 128), HEADS_HERE * QW)],
            qbuf.at[shard, pl.ds(pl.multiple_of(slot * NEW, 16), NEW), :],
            q_s.at[shard, lax.rem(d + SEQ, SEQ)], q_r.at[shard, lax.rem(d + SEQ, SEQ)],
            device_id={"seq": z}, device_id_type=MESH,
        )

    q_away = (1, -1, 2, -2, 3, -3, 8 * odd - 4)

    def q_start(shard):
        head_shard = lax.rem(me + 8 * shard, SEQ)
        slot = -first_of(me)
        pltpu.make_async_copy(
            q_hbm.at[:, pl.ds(pl.multiple_of(head_shard * (HEADS_HERE * QW), 128), HEADS_HERE * QW)],
            qbuf.at[shard, pl.ds(pl.multiple_of(slot * NEW, 16), NEW), :], loc_q.at[shard],
        ).start()
        for d in q_away:
            q_copy(shard, d).start()

    def q_wait(shard):
        pltpu.make_async_copy(
            q_hbm.at[:, 0 : HEADS_HERE * QW], qbuf.at[shard, 0:NEW, :], loc_q.at[shard]
        ).wait()
        for d in (1, -1, 2, -2, 3, -3, 8 * odd - 4):
            q_copy(shard, d).wait_recv()

    q_start(0)

    far_w.wait_recv()

    def w_copy(d):
        return pltpu.make_async_remote_copy(
            wbuf.at[1, my_slice, :], wbuf.at[1, my_slice, :], w2_s.at[d], w2_r.at[d],
            device_id={"rep": lax.rem(rep + d, reps)}, device_id_type=MESH,
        )

    def spread(d, c):
        w_copy(d).start()
        return c

    lax.fori_loop(1, reps, spread, 0)
    q_start(1)

    pr = lax.broadcasted_iota(jnp.int32, (2 * QW, 512), 0)
    pc = lax.broadcasted_iota(jnp.int32, (2 * QW, 512), 1)
    want = jnp.where(pc < 256, jnp.where(pc < QW, pc, -1), jnp.where(pc < 256 + QW, pc - 256 + QW, -1))
    perm[...] = jnp.where(pr == want, 1.0, 0.0).astype(BF)
    sr = lax.broadcasted_iota(jnp.int32, (128, 256), 0)
    sc = lax.broadcasted_iota(jnp.int32, (128, 256), 1)
    want = jnp.where(sc < 128, jnp.where(sc < ROPE, sc, -1), jnp.where(sc < 128 + ROPE, sc - 128 + ROPE, -1))
    sel[...] = jnp.where(sr == want, 1.0, 0.0).astype(BF)
    row = lax.broadcasted_iota(jnp.int32, (ROWS, SEQ * NEW), 0)
    col = lax.broadcasted_iota(jnp.int32, (ROWS, SEQ * NEW), 1)
    token = row + (me + first_of(me) + SEQ) * NEW
    token = jnp.where(token >= 2 * SEQ * NEW, token - 2 * SEQ * NEW, jnp.where(token >= SEQ * NEW, token - SEQ * NEW, token))
    bias[...] = jnp.where(col <= token, 0.0, -jnp.inf)

    def put(ref, head, src, val):
        ref[head, pl.ds(pl.multiple_of(src * PRE, 16), PRE), :] = val[0:PRE]
        ref[head, pl.ds(pl.multiple_of(PRE_ALL + src * NEW, 16), NEW), :] = val[PRE:]

    def project(shard, srcs, heads):
        x = [lat[s, 0:128, :] for s in srcs]
        x = x[0] if len(x) == 1 else jnp.concatenate(x, axis=0)
        for h in heads:
            kv = mm(x, wbuf[shard, :, SPAN * h : SPAN * h + SPAN]).astype(BF)
            for n, s in enumerate(srcs):
                put(kbuf, shard * HEADS_HERE + h, s, kv[128 * n : 128 * n + 128, 0:NOPE])
                put(vbuf, shard * HEADS_HERE + h, s, kv[128 * n : 128 * n + 128, NOPE:])

    def unpack_rope(src):
        for t in range(4):
            pair = mm(lat[src, 128:CHUNK, 128 * t : 128 * t + 128], sel[...]).astype(BF)
            ropes[pl.ds(pl.multiple_of(src * PRE + 32 * t, 16), 16), :] = pair[:, 0:128]
            high = src * PRE + 32 * t + 16 if t < 3 else PRE_ALL + src * NEW
            ropes[pl.ds(pl.multiple_of(high, 16), 16), :] = pair[:, 128:]

    own_w.wait()
    parts = ((0, 1, 2), (3, 4, 5), (6, 7))

    def ring_step(step, last):
        for j in range(3):
            for way in (0, 1):
                ring_in(way, step - 1, subs[j], j).wait_recv()
                if not last:
                    ring(way, step, subs[j], j).start()
            if last and j == 1:
                ring(0, step, halves[0], 0).start()
            if last and j == 2:
                ring(1, step, halves[1], 0).start()
            srcs = (at(1 - step), at(step - 1))
            project(0, srcs, parts[j])
            if j == 2:
                unpack_rope(srcs[0])
                unpack_rope(srcs[1])

    def loop_step(step, c):
        ring_step(step, False)
        return c

    lax.fori_loop(1, 7, loop_step, 0)
    ring_step(7, True)
    srcs = (at(-7), at(7))
    project(0, srcs, range(HEADS_HERE))
    unpack_rope(srcs[0])
    unpack_rope(srcs[1])
    ring_in(0, 7, halves[0], 0).wait_recv()
    ring_in(1, 7, halves[1], 0).wait_recv()
    project(0, (at(8),), range(HEADS_HERE))
    unpack_rope(at(8))

    factor = math.log2(math.e) / math.sqrt(QW)
    o_away = (1, -1, 2, -2, 3, -3, 4 - 8 * odd)

    def o_copy(shard, pair, d):
        slot = d - first_of(me)
        cols = lax.rem(me + 8 * shard, SEQ) * (HEADS_HERE * VDIM) + pair * (2 * VDIM)
        return pltpu.make_async_remote_copy(
            obuf.at[shard * 4 + pair, pl.ds(pl.multiple_of(slot * NEW, 16), NEW), :],
            out_hbm.at[:, pl.ds(pl.multiple_of(cols, 128), 2 * VDIM)],
            o_s.at[shard, pair, lax.rem(d + SEQ, SEQ)], o_r.at[shard, pair, lax.rem(d + SEQ, SEQ)],
            device_id={"seq": at(d)}, device_id_type=MESH,
        )

    def o_local(shard, pair):
        slot = -first_of(me)
        cols = lax.rem(me + 8 * shard, SEQ) * (HEADS_HERE * VDIM) + pair * (2 * VDIM)
        return pltpu.make_async_copy(
            obuf.at[shard * 4 + pair, pl.ds(pl.multiple_of(slot * NEW, 16), NEW), :],
            out_hbm.at[:, pl.ds(pl.multiple_of(cols, 128), 2 * VDIM)], loc_o.at[shard, pair],
        )

    def attend(shard, pair):
        qp = qbuf[shard, :, pl.ds(pl.multiple_of(pair * (2 * QW), 128), 2 * QW)]
        qp = mm(qp, perm[...]).astype(BF)
        for n in range(2):
            head = shard * HEADS_HERE + 2 * pair + n
            keys = jnp.concatenate([kbuf[head], ropes[...]], axis=1)
            s = mm_t(qp[:, 256 * n : 256 * n + 256], keys)
            s = jnp.concatenate([s[:, 0:PRE_ALL], s[:, PRE_ALL:] + bias[...]], axis=1)
            top = jnp.max(s, axis=1, keepdims=True)
            e = jnp.exp2((s - top) * factor)
            total = jnp.sum(e, axis=1, keepdims=True)
            o = mm(e.astype(BF), vbuf[head]) / total
            obuf[shard * 4 + pair, :, VDIM * n : VDIM * n + VDIM] = o.astype(BF)
        o_local(shard, pair).start()
        for d in o_away:
            o_copy(shard, pair, d).start()

    def attend_all(shard):
        def step(pair, c):
            attend(shard, pair)
            return c

        lax.fori_loop(0, 4, step, 0)

    q_wait(0)
    attend_all(0)

    def w_wait(d, c):
        w_copy(d).wait_recv()
        return c

    lax.fori_loop(1, reps, w_wait, 0)

    def far_project(i, c):
        project(1, (2 * i, 2 * i + 1), range(HEADS_HERE))
        return c

    lax.fori_loop(0, SEQ // 2, far_project, 0)
    q_wait(1)
    attend_all(1)

    for shard in (0, 1):
        for d in q_away:
            q_copy(shard, d).wait_send()

        def o_wait(pair, c):
            o_local(shard, pair).wait()
            for d in o_away:
                o_copy(shard, pair, d).wait_send()
                o_copy(shard, pair, d).wait_recv()
            return c

        lax.fori_loop(0, 4, o_wait, 0)
    far_w.wait_send()

    def w_sent(d, c):
        w_copy(d).wait_send()
        return c

    lax.fori_loop(1, reps, w_sent, 0)

    def ring_sent(step, c):
        for way in (0, 1):
            for j in range(3):
                ring(way, step, subs[j], j).wait_send()
        return c

    lax.fori_loop(0, 7, ring_sent, 0)
    for way in (0, 1):
        ring(way, 7, halves[way], 0).wait_send()


def body(queries, stretch_latent, prefix_latent, kv_up_weight):
    reps = lax.axis_size("rep")
    dma = pltpu.SemaphoreType.DMA
    hbm = pl.BlockSpec(memory_space=pl.ANY)
    vmem = pl.BlockSpec(memory_space=pltpu.VMEM)
    return pl.pallas_call(
        functools.partial(kernel, reps),
        out_shape=jax.ShapeDtypeStruct((NEW, SEQ * HEADS_HERE * VDIM), BF),
        in_specs=[vmem, vmem, hbm, hbm],
        out_specs=hbm,
        scratch_shapes=[
            pltpu.VMEM((SEQ, CHUNK, KV_RANK), BF),
            pltpu.VMEM((2, ROWS, HEADS_HERE * QW), BF),
            pltpu.VMEM((2, KV_RANK, HEADS_HERE * SPAN), BF),
            pltpu.VMEM((2 * HEADS_HERE, KEYS, NOPE), BF),
            pltpu.VMEM((2 * HEADS_HERE, KEYS, VDIM), BF),
            pltpu.VMEM((KEYS, 128), BF),
            pltpu.VMEM((HEADS_HERE, ROWS, 2 * VDIM), BF),
            pltpu.VMEM((2 * QW, 512), BF),
            pltpu.VMEM((128, 256), BF),
            pltpu.VMEM((ROWS, SEQ * NEW), F32),
            dma((2, 8, 3)), dma((2, 8, 3)),
            dma((2, SEQ)), dma((2, SEQ)),
            dma((2, 4, SEQ)), dma((2, 4, SEQ)),
            dma, dma, dma((reps,)), dma((reps,)),
            dma, dma((2,)), dma((2, 4)),
        ],
        compiler_params=pltpu.CompilerParams(
            collective_id=0, has_side_effects=True, vmem_limit_bytes=60 * 1024 * 1024
        ),
        cost_estimate=pl.CostEstimate(flops=13_000_000_000, bytes_accessed=8_000_000, transcendentals=4_200_000),
    )(prefix_latent, stretch_latent, queries, kv_up_weight)


def solution(mesh):
    in_specs = (
        P(("rep", "seq"), None),
        P(("rep", "seq"), None),
        P(("rep", "seq"), None),
        P(None, "seq"),
    )
    out_specs = P(("rep", "seq"), None)
    return jax.shard_map(body, mesh=mesh, in_specs=in_specs, out_specs=out_specs, check_vma=False)
```

```python
import functools
import math

import jax
import jax.numpy as jnp
from jax import lax
from jax.experimental import pallas as pl
from jax.experimental.pallas import tpu as pltpu
from jax.sharding import PartitionSpec as P

KV_RANK = 512
ROPE = 64
NOPE = 128
VDIM = 128
QW = NOPE + ROPE
SPAN = NOPE + VDIM
SEQ = 16
HEADS_HERE = 8
PRE = 112
NEW = 16
KEYS = SEQ * (PRE + NEW)
PRE_ALL = SEQ * PRE
WINDOW = 8
ROWS = WINDOW * NEW
CHUNK = 144
SUB = 48
HALF_AT = 5
FAR_AT = 6
FAR_UNITS = 6 // (7 - FAR_AT)
Q1_FROM = 5
MESH = pl.DeviceIdType.MESH
BF = jnp.bfloat16
F32 = jnp.float32


def mm(a, b):
    return jnp.dot(a, b, preferred_element_type=F32)


def mm_t(a, b):
    return lax.dot_general(a, b, (((1,), (1,)), ((), ())), preferred_element_type=F32)


def kernel(
    reps, prefix_hbm, stretch_hbm, q_hbm, w_hbm, out_hbm,
    own, lat, qbuf, wbuf, kbuf, vbuf, ropes, obuf, perm, sel, bias,
    ring_s, ring_r, q_s, q_r, o_s, o_r, w1_s, w1_r, w2_s, w2_r, w3_s, w3_r, loc_w, loc_x, loc_q, loc_o,
):
    me = lax.axis_index("seq")
    rep = lax.axis_index("rep")
    odd = lax.rem(me, 2)
    chips = reps // 2
    core = lax.rem(rep, 2)
    sibling = rep + 1 - 2 * core
    slice_rows = KV_RANK // reps

    def at(d):
        return lax.rem(me + d + 2 * SEQ, SEQ)

    def first_of(z):
        return -3 - lax.rem(z, 2)

    barrier = pltpu.get_barrier_semaphore()
    z_partners = (1, -1, 2, -2, 3, -3, 4, -4, 8)
    for d in z_partners:
        pl.semaphore_signal(barrier, inc=1, device_id={"seq": at(d)}, device_id_type=MESH)

    def greet(d, c):
        pl.semaphore_signal(barrier, inc=1, device_id={"rep": lax.rem(rep + 2 * d, reps)}, device_id_type=MESH)
        return c

    lax.fori_loop(1, chips, greet, 0)
    pl.semaphore_signal(barrier, inc=1, device_id={"rep": sibling}, device_id_type=MESH)

    own_prefix = pltpu.make_async_copy(prefix_hbm, own.at[0:PRE, :], loc_x.at[0])
    own_stretch = pltpu.make_async_copy(stretch_hbm, own.at[PRE : PRE + NEW, :], loc_x.at[1])
    own_w = pltpu.make_async_copy(w_hbm, wbuf.at[0], loc_w)
    own_prefix.start()
    own_stretch.start()
    own_w.start()
    r64 = lax.broadcasted_iota(jnp.int32, (ROPE, 128), 0)
    c64 = lax.broadcasted_iota(jnp.int32, (ROPE, 128), 1)
    put_low = jnp.where(c64 == r64, 1.0, 0.0).astype(BF)
    put_high = jnp.where(c64 == r64 + ROPE, 1.0, 0.0).astype(BF)
    own_prefix.wait()
    own_stretch.wait()
    lat[me, 0:128, :] = own[:, 0:KV_RANK]
    low = mm(own[:, KV_RANK:], put_low)
    high = mm(own[:, KV_RANK:], put_high)
    for t in range(4):
        lat[me, 128:CHUNK, 128 * t : 128 * t + 128] = (
            low[32 * t : 32 * t + 16] + high[32 * t + 16 : 32 * t + 32]
        ).astype(BF)

    pl.semaphore_wait(barrier, len(z_partners) + chips)

    my_slice = pl.ds(pl.multiple_of((core * chips + rep // 2) * slice_rows, 16), slice_rows)
    far_w = pltpu.make_async_remote_copy(
        w_hbm.at[my_slice, :], wbuf.at[1, my_slice, :], w1_s, w1_r, device_id={"seq": at(8)}, device_id_type=MESH
    )
    far_w.start()

    def ring_copy(held, way, step, rows, j):
        ref = lat.at[held, rows]
        return pltpu.make_async_remote_copy(
            ref, ref, ring_s.at[way, step, j], ring_r.at[way, step, j],
            device_id={"seq": at(1) if way == 0 else at(-1)}, device_id_type=MESH,
        )

    def ring(way, step, rows, j):
        return ring_copy(at(-step) if way == 0 else at(step), way, step, rows, j)

    def ring_in(way, step, rows, j):
        return ring_copy(at(-step - 1) if way == 0 else at(step + 1), way, step, rows, j)

    subs = [pl.ds(j * SUB, SUB) for j in range(3)]
    halves = [pl.ds(0, 80), pl.ds(80, 64)]
    for j in range(3):
        for way in (0, 1):
            ring(way, 0, subs[j], j).start()

    def q_copy(shard, d):
        z = at(d)
        head_shard = lax.rem(z + 8 * shard, SEQ)
        slot = -d - first_of(z)
        return pltpu.make_async_remote_copy(
            q_hbm.at[:, pl.ds(pl.multiple_of(head_shard * (HEADS_HERE * QW), 128), HEADS_HERE * QW)],
            qbuf.at[shard, pl.ds(pl.multiple_of(slot * NEW, 16), NEW), :],
            q_s.at[shard, lax.rem(d + SEQ, SEQ)], q_r.at[shard, lax.rem(d + SEQ, SEQ)],
            device_id={"seq": z}, device_id_type=MESH,
        )

    def q_own(shard):
        head_shard = lax.rem(me + 8 * shard, SEQ)
        slot = -first_of(me)
        return pltpu.make_async_copy(
            q_hbm.at[:, pl.ds(pl.multiple_of(head_shard * (HEADS_HERE * QW), 128), HEADS_HERE * QW)],
            qbuf.at[shard, pl.ds(pl.multiple_of(slot * NEW, 16), NEW), :], loc_q.at[shard],
        )

    q_farthest = 8 * odd - 4
    q_away = (1, -1, 2, -2, 3, -3, q_farthest)

    def nth(i):
        return (1 - 2 * lax.rem(i, 2)) * (i // 2 + 1)

    def q_wait(shard):
        q_own(shard).wait()
        for d in q_away:
            q_copy(shard, d).wait_recv()

    q_own(0).start()
    q_own(1).start()
    q_copy(0, q_farthest).start()

    def w_copy(d):
        return pltpu.make_async_remote_copy(
            wbuf.at[1, my_slice, :], wbuf.at[1, my_slice, :], w2_s.at[d], w2_r.at[d],
            device_id={"rep": lax.rem(rep + 2 * d, reps)}, device_id_type=MESH,
        )

    my_half = pl.ds(pl.multiple_of(core * (KV_RANK // 2), 16), KV_RANK // 2)
    half_w = pltpu.make_async_remote_copy(
        wbuf.at[1, my_half, :], wbuf.at[1, my_half, :], w3_s, w3_r, device_id={"rep": sibling}, device_id_type=MESH
    )

    def spread(d, c):
        w_copy(d).start()
        return c

    def w_wait(d, c):
        w_copy(d).wait_recv()
        return c

    pr = lax.broadcasted_iota(jnp.int32, (2 * QW, 512), 0)
    pc = lax.broadcasted_iota(jnp.int32, (2 * QW, 512), 1)
    want = jnp.where(pc < 256, jnp.where(pc < QW, pc, -1), jnp.where(pc < 256 + QW, pc - 256 + QW, -1))
    perm[...] = jnp.where(pr == want, 1.0, 0.0).astype(BF)
    sr = lax.broadcasted_iota(jnp.int32, (128, 256), 0)
    sc = lax.broadcasted_iota(jnp.int32, (128, 256), 1)
    want = jnp.where(sc < 128, jnp.where(sc < ROPE, sc, -1), jnp.where(sc < 128 + ROPE, sc - 128 + ROPE, -1))
    sel[...] = jnp.where(sr == want, 1.0, 0.0).astype(BF)
    row = lax.broadcasted_iota(jnp.int32, (ROWS, SEQ * NEW), 0)
    col = lax.broadcasted_iota(jnp.int32, (ROWS, SEQ * NEW), 1)
    token = row + (me + first_of(me) + SEQ) * NEW
    token = jnp.where(token >= 2 * SEQ * NEW, token - 2 * SEQ * NEW, jnp.where(token >= SEQ * NEW, token - SEQ * NEW, token))
    bias[...] = jnp.where(col <= token, 0.0, -jnp.inf)

    def put(ref, head, src, val):
        ref[head, pl.ds(pl.multiple_of(src * PRE, 16), PRE), :] = val[0:PRE]
        ref[head, pl.ds(pl.multiple_of(PRE_ALL + src * NEW, 16), NEW), :] = val[PRE:]

    def project(shard, srcs):
        x = [lat[s, 0:128, :] for s in srcs]
        x = x[0] if len(x) == 1 else jnp.concatenate(x, axis=0)
        for h in range(HEADS_HERE):
            kv = mm(x, wbuf[shard, :, SPAN * h : SPAN * h + SPAN]).astype(BF)
            for n, s in enumerate(srcs):
                put(kbuf, shard * HEADS_HERE + h, s, kv[128 * n : 128 * n + 128, 0:NOPE])
                put(vbuf, shard * HEADS_HERE + h, s, kv[128 * n : 128 * n + 128, NOPE:])

    def unpack_rope(src):
        for t in range(4):
            pair = mm(lat[src, 128:CHUNK, 128 * t : 128 * t + 128], sel[...]).astype(BF)
            ropes[pl.ds(pl.multiple_of(src * PRE + 32 * t, 16), 16), :] = pair[:, 0:128]
            high = src * PRE + 32 * t + 16 if t < 3 else PRE_ALL + src * NEW
            ropes[pl.ds(pl.multiple_of(high, 16), 16), :] = pair[:, 128:]

    def both(i):
        return at(-i), at(i)

    def ring_step(step, c):
        for j in range(3):
            for way in (0, 1):
                ring_in(way, step - 1, subs[j], j).wait_recv()
                ring(way, step, subs[j], j).start()
            if j == 0:
                q_copy(0, nth(step - 1)).start()

                @pl.when(step == 1)
                def _():
                    own_w.wait()

            if j == 1:
                project(0, both(step - 1))
                for s in both(step - 1):
                    unpack_rope(s)

        @pl.when(step == 1)
        def _():
            far_w.wait_recv()
            lax.fori_loop(1, chips, spread, 0)

        @pl.when(step == HALF_AT)
        def _():
            lax.fori_loop(1, chips, w_wait, 0)
            half_w.start()

        @pl.when(step >= Q1_FROM)
        def _():
            q_copy(1, nth(step - Q1_FROM)).start()

        @pl.when(step >= FAR_AT)
        def _():
            @pl.when(step == FAR_AT)
            def _():
                half_w.wait_recv()

            def unit(i, c):
                project(1, both((step - FAR_AT) * FAR_UNITS + i))
                return c

            lax.fori_loop(0, FAR_UNITS, unit, 0)

        return c

    lax.fori_loop(1, 7, ring_step, 0)
    for j in range(3):
        for way in (0, 1):
            ring_in(way, 6, subs[j], j).wait_recv()
        if j > 0:
            ring(j - 1, 7, halves[j - 1], 0).start()
    for i in range(7 - Q1_FROM, 6):
        q_copy(1, nth(i)).start()
    q_copy(1, q_farthest).start()

    def rest(i, c):
        project(lax.rem(i, 2), both(6 + i // 2))
        return c

    lax.fori_loop(0, 4, rest, 0)
    for i in (6, 7):
        for s in both(i):
            unpack_rope(s)
    for way in (0, 1):
        ring_in(way, 7, halves[way], 0).wait_recv()

    def last(shard, c):
        project(shard, (at(8),))
        return c

    lax.fori_loop(0, 2, last, 0)
    unpack_rope(at(8))

    factor = math.log2(math.e) / math.sqrt(QW)
    o_away = (1, -1, 2, -2, 3, -3, 4 - 8 * odd)

    def o_place(shard, pair, slot):
        cols = lax.rem(me + 8 * shard, SEQ) * (HEADS_HERE * VDIM) + pair * (2 * VDIM)
        return (
            obuf.at[shard * 4 + pair, pl.ds(pl.multiple_of(slot * NEW, 16), NEW), :],
            out_hbm.at[:, pl.ds(pl.multiple_of(cols, 128), 2 * VDIM)],
        )

    def o_copy(shard, pair, d):
        src, dst = o_place(shard, pair, d - first_of(me))
        return pltpu.make_async_remote_copy(
            src, dst, o_s.at[shard, pair, lax.rem(d + SEQ, SEQ)], o_r.at[shard, pair, lax.rem(d + SEQ, SEQ)],
            device_id={"seq": at(d)}, device_id_type=MESH,
        )

    def o_own(shard, pair):
        src, dst = o_place(shard, pair, -first_of(me))
        return pltpu.make_async_copy(src, dst, loc_o.at[shard, pair])

    def attend(i, c):
        shard, pair = i // 4, lax.rem(i, 4)

        @pl.when(i == 0)
        def _():
            q_wait(0)

        @pl.when(i == 4)
        def _():
            q_wait(1)

        qp = qbuf[shard, :, pl.ds(pl.multiple_of(pair * (2 * QW), 128), 2 * QW)]
        qp = mm(qp, perm[...]).astype(BF)
        for n in range(2):
            head = shard * HEADS_HERE + 2 * pair + n
            keys = jnp.concatenate([kbuf[head], ropes[...]], axis=1)
            s = mm_t(qp[:, 256 * n : 256 * n + 256], keys)
            s = jnp.concatenate([s[:, 0:PRE_ALL], s[:, PRE_ALL:] + bias[...]], axis=1)
            top = jnp.max(s, axis=1, keepdims=True)
            e = jnp.exp2((s - top) * factor)
            total = jnp.sum(e, axis=1, keepdims=True)
            o = mm(e.astype(BF), vbuf[head]) / total
            obuf[i, :, VDIM * n : VDIM * n + VDIM] = o.astype(BF)
        o_own(shard, pair).start()
        for d in o_away:
            o_copy(shard, pair, d).start()
        return c

    lax.fori_loop(0, 8, attend, 0)

    def o_wait(i, c):
        shard, pair = i // 4, lax.rem(i, 4)
        o_own(shard, pair).wait()
        for d in o_away:
            o_copy(shard, pair, d).wait_send()
            o_copy(shard, pair, d).wait_recv()
        return c

    lax.fori_loop(0, 8, o_wait, 0)
    for shard in (0, 1):
        for d in q_away:
            q_copy(shard, d).wait_send()
    far_w.wait_send()

    def w_sent(d, c):
        w_copy(d).wait_send()
        return c

    lax.fori_loop(1, chips, w_sent, 0)
    half_w.wait_send()

    def ring_sent(step, c):
        for way in (0, 1):
            for j in range(3):
                ring(way, step, subs[j], j).wait_send()
        return c

    lax.fori_loop(0, 7, ring_sent, 0)
    for way in (0, 1):
        ring(way, 7, halves[way], 0).wait_send()


def body(queries, stretch_latent, prefix_latent, kv_up_weight):
    reps = lax.axis_size("rep")
    dma = pltpu.SemaphoreType.DMA
    hbm = pl.BlockSpec(memory_space=pltpu.HBM)
    return pl.pallas_call(
        functools.partial(kernel, reps),
        out_shape=jax.ShapeDtypeStruct((NEW, SEQ * HEADS_HERE * VDIM), BF),
        in_specs=[hbm] * 4,
        out_specs=pl.BlockSpec(memory_space=pl.ANY),
        scratch_shapes=[
            pltpu.VMEM((PRE + NEW, KV_RANK + ROPE), BF),
            pltpu.VMEM((SEQ, CHUNK, KV_RANK), BF),
            pltpu.VMEM((2, ROWS, HEADS_HERE * QW), BF),
            pltpu.VMEM((2, KV_RANK, HEADS_HERE * SPAN), BF),
            pltpu.VMEM((2 * HEADS_HERE, KEYS, NOPE), BF),
            pltpu.VMEM((2 * HEADS_HERE, KEYS, VDIM), BF),
            pltpu.VMEM((KEYS, 128), BF),
            pltpu.VMEM((HEADS_HERE, ROWS, 2 * VDIM), BF),
            pltpu.VMEM((2 * QW, 512), BF),
            pltpu.VMEM((128, 256), BF),
            pltpu.VMEM((ROWS, SEQ * NEW), F32),
            dma((2, 8, 3)), dma((2, 8, 3)),
            dma((2, SEQ)), dma((2, SEQ)),
            dma((2, 4, SEQ)), dma((2, 4, SEQ)),
            dma, dma, dma((reps // 2,)), dma((reps // 2,)), dma, dma,
            dma, dma((2,)), dma((2,)), dma((2, 4)),
        ],
        compiler_params=pltpu.CompilerParams(
            collective_id=0, has_side_effects=True, vmem_limit_bytes=60 * 1024 * 1024
        ),
        cost_estimate=pl.CostEstimate(flops=13_000_000_000, bytes_accessed=8_000_000, transcendentals=4_200_000),
    )(prefix_latent, stretch_latent, queries, kv_up_weight)


def solution(mesh):
    in_specs = (
        P(("rep", "seq"), None),
        P(("rep", "seq"), None),
        P(("rep", "seq"), None),
        P(None, "seq"),
    )
    out_specs = P(("rep", "seq"), None)
    return jax.shard_map(body, mesh=mesh, in_specs=in_specs, out_specs=out_specs, check_vma=False)
```

```python
import functools
import math

import jax
import jax.numpy as jnp
from jax import lax
from jax.experimental import pallas as pl
from jax.experimental.pallas import tpu as pltpu
from jax.sharding import PartitionSpec as P

KV_RANK = 512
ROPE = 64
NOPE = 128
VDIM = 128
QW = NOPE + ROPE
SPAN = NOPE + VDIM
SEQ = 16
HEADS_HERE = 8
PRE = 112
NEW = 16
KEYS = SEQ * (PRE + NEW)
PRE_ALL = SEQ * PRE
WINDOW = 8
ROWS = WINDOW * NEW
CHUNK = 144
SUB = 48
HALF_AT = 5
FAR_AT = 6
FAR_UNITS = 6 // (7 - FAR_AT)
Q1_FROM = 5
MESH = pl.DeviceIdType.MESH
BF = jnp.bfloat16
F32 = jnp.float32


def mm(a, b):
    return jnp.dot(a, b, preferred_element_type=F32)


def mm_t(a, b):
    return lax.dot_general(a, b, (((1,), (1,)), ((), ())), preferred_element_type=F32)


def kernel(
    reps, prefix_hbm, stretch_hbm, q_hbm, w_hbm, out_hbm,
    own, lat, qbuf, wbuf, kbuf, vbuf, ropes, obuf, perm, sel, bias,
    ring_s, ring_r, q_s, q_r, o_s, o_r, w1_s, w1_r, w2_s, w2_r, w3_s, w3_r, loc_w, loc_x, loc_q, loc_o,
):
    me = lax.axis_index("seq")
    rep = lax.axis_index("rep")
    odd = lax.rem(me, 2)
    chips = reps // 2
    core = lax.rem(rep, 2)
    sibling = rep + 1 - 2 * core
    slice_rows = KV_RANK // reps

    def at(d):
        return lax.rem(me + d + 2 * SEQ, SEQ)

    def first_of(z):
        return lax.rem(z, 2) - 4

    def shard_of(z, shard):
        return lax.rem(z + shard * (7 + 2 * lax.rem(z, 2)), SEQ)

    own_prefix = pltpu.make_async_copy(prefix_hbm, own.at[0:PRE, :], loc_x.at[0])
    own_stretch = pltpu.make_async_copy(stretch_hbm, own.at[PRE : PRE + NEW, :], loc_x.at[1])
    own_w = pltpu.make_async_copy(w_hbm, wbuf.at[0], loc_w)
    own_prefix.start()
    own_stretch.start()

    barrier = pltpu.get_barrier_semaphore()
    far = 7 - 14 * odd
    z_partners = (1, -1, 2, -2, 3, -3, 4, -4, far)
    for d in z_partners:
        pl.semaphore_signal(barrier, inc=1, device_id={"seq": at(d)}, device_id_type=MESH)

    def greet(d, c):
        pl.semaphore_signal(barrier, inc=1, device_id={"rep": lax.rem(rep + 2 * d, reps)}, device_id_type=MESH)
        return c

    lax.fori_loop(1, chips, greet, 0)
    pl.semaphore_signal(barrier, inc=1, device_id={"rep": sibling}, device_id_type=MESH)

    own_w.start()
    r64 = lax.broadcasted_iota(jnp.int32, (ROPE, 128), 0)
    c64 = lax.broadcasted_iota(jnp.int32, (ROPE, 128), 1)
    put_low = jnp.where(c64 == r64, 1.0, 0.0).astype(BF)
    put_high = jnp.where(c64 == r64 + ROPE, 1.0, 0.0).astype(BF)
    own_prefix.wait()
    own_stretch.wait()
    lat[me, 0:128, :] = own[:, 0:KV_RANK]
    pl.semaphore_wait(barrier, len(z_partners) + chips)

    my_slice = pl.ds(pl.multiple_of((core * chips + rep // 2) * slice_rows, 16), slice_rows)
    far_w = pltpu.make_async_remote_copy(
        w_hbm.at[my_slice, :], wbuf.at[1, my_slice, :], w1_s, w1_r, device_id={"seq": at(far)}, device_id_type=MESH
    )
    far_w.start()

    def ring_copy(held, way, step, rows, j):
        ref = lat.at[held, rows]
        return pltpu.make_async_remote_copy(
            ref, ref, ring_s.at[way, step, j], ring_r.at[way, step, j],
            device_id={"seq": at(1) if way == 0 else at(-1)}, device_id_type=MESH,
        )

    def ring(way, step, rows, j):
        return ring_copy(at(-step) if way == 0 else at(step), way, step, rows, j)

    def ring_in(way, step, rows, j):
        return ring_copy(at(-step - 1) if way == 0 else at(step + 1), way, step, rows, j)

    subs = [pl.ds(j * SUB, SUB) for j in range(3)]
    halves = [pl.ds(0, 80), pl.ds(80, 64)]
    for j in range(3):
        if j == 2:
            low = mm(own[:, KV_RANK:], put_low)
            high = mm(own[:, KV_RANK:], put_high)
            for t in range(4):
                lat[me, 128:CHUNK, 128 * t : 128 * t + 128] = (
                    low[32 * t : 32 * t + 16] + high[32 * t + 16 : 32 * t + 32]
                ).astype(BF)
        for way in (0, 1):
            ring(way, 0, subs[j], j).start()

    def q_copy(shard, d):
        z = at(d)
        head_shard = shard_of(z, shard)
        slot = -d - first_of(z)
        return pltpu.make_async_remote_copy(
            q_hbm.at[:, pl.ds(pl.multiple_of(head_shard * (HEADS_HERE * QW), 128), HEADS_HERE * QW)],
            qbuf.at[shard, pl.ds(pl.multiple_of(slot * NEW, 16), NEW), :],
            q_s.at[shard, lax.rem(d + SEQ, SEQ)], q_r.at[shard, lax.rem(d + SEQ, SEQ)],
            device_id={"seq": z}, device_id_type=MESH,
        )

    def q_own(shard):
        head_shard = shard_of(me, shard)
        slot = -first_of(me)
        return pltpu.make_async_copy(
            q_hbm.at[:, pl.ds(pl.multiple_of(head_shard * (HEADS_HERE * QW), 128), HEADS_HERE * QW)],
            qbuf.at[shard, pl.ds(pl.multiple_of(slot * NEW, 16), NEW), :], loc_q.at[shard],
        )

    q_farthest = 4 - 8 * odd
    q_away = (1, -1, 2, -2, 3, -3, q_farthest)

    def nth(i):
        return (1 - 2 * lax.rem(i, 2)) * (i // 2 + 1)

    def q_wait(shard):
        q_own(shard).wait()
        for d in q_away:
            q_copy(shard, d).wait_recv()

    q_own(0).start()
    q_own(1).start()
    q_copy(0, q_farthest).start()

    def w_copy(d):
        return pltpu.make_async_remote_copy(
            wbuf.at[1, my_slice, :], wbuf.at[1, my_slice, :], w2_s.at[d], w2_r.at[d],
            device_id={"rep": lax.rem(rep + 2 * d, reps)}, device_id_type=MESH,
        )

    my_half = pl.ds(pl.multiple_of(core * (KV_RANK // 2), 16), KV_RANK // 2)
    half_w = pltpu.make_async_remote_copy(
        wbuf.at[1, my_half, :], wbuf.at[1, my_half, :], w3_s, w3_r, device_id={"rep": sibling}, device_id_type=MESH
    )

    def spread(d, c):
        w_copy(d).start()
        return c

    def w_wait(d, c):
        w_copy(d).wait_recv()
        return c

    pr = lax.broadcasted_iota(jnp.int32, (2 * QW, 512), 0)
    pc = lax.broadcasted_iota(jnp.int32, (2 * QW, 512), 1)
    want = jnp.where(pc < 256, jnp.where(pc < QW, pc, -1), jnp.where(pc < 256 + QW, pc - 256 + QW, -1))
    perm[...] = jnp.where(pr == want, 1.0, 0.0).astype(BF)
    sr = lax.broadcasted_iota(jnp.int32, (128, 256), 0)
    sc = lax.broadcasted_iota(jnp.int32, (128, 256), 1)
    want = jnp.where(sc < 128, jnp.where(sc < ROPE, sc, -1), jnp.where(sc < 128 + ROPE, sc - 128 + ROPE, -1))
    sel[...] = jnp.where(sr == want, 1.0, 0.0).astype(BF)
    row = lax.broadcasted_iota(jnp.int32, (ROWS, SEQ * NEW), 0)
    col = lax.broadcasted_iota(jnp.int32, (ROWS, SEQ * NEW), 1)
    token = row + (me + first_of(me) + SEQ) * NEW
    token = jnp.where(token >= 2 * SEQ * NEW, token - 2 * SEQ * NEW, jnp.where(token >= SEQ * NEW, token - SEQ * NEW, token))
    bias[...] = jnp.where(col <= token, 0.0, -jnp.inf)

    def put(ref, head, src, val):
        ref[head, pl.ds(pl.multiple_of(src * PRE, 16), PRE), :] = val[0:PRE]
        ref[head, pl.ds(pl.multiple_of(PRE_ALL + src * NEW, 16), NEW), :] = val[PRE:]

    def project(shard, srcs):
        x = [lat[s, 0:128, :] for s in srcs]
        x = x[0] if len(x) == 1 else jnp.concatenate(x, axis=0)
        for h in range(HEADS_HERE):
            kv = mm(x, wbuf[shard, :, SPAN * h : SPAN * h + SPAN]).astype(BF)
            for n, s in enumerate(srcs):
                put(kbuf, shard * HEADS_HERE + h, s, kv[128 * n : 128 * n + 128, 0:NOPE])
                put(vbuf, shard * HEADS_HERE + h, s, kv[128 * n : 128 * n + 128, NOPE:])

    def unpack_rope(src):
        for t in range(4):
            pair = mm(lat[src, 128:CHUNK, 128 * t : 128 * t + 128], sel[...]).astype(BF)
            ropes[pl.ds(pl.multiple_of(src * PRE + 32 * t, 16), 16), :] = pair[:, 0:128]
            high = src * PRE + 32 * t + 16 if t < 3 else PRE_ALL + src * NEW
            ropes[pl.ds(pl.multiple_of(high, 16), 16), :] = pair[:, 128:]

    def both(i):
        return at(-i), at(i)

    def ring_step(step, c):
        for j in range(3):
            for way in (0, 1):
                ring_in(way, step - 1, subs[j], j).wait_recv()
                ring(way, step, subs[j], j).start()
            if j == 0:
                q_copy(0, nth(step - 1)).start()

                @pl.when(step == 1)
                def _():
                    own_w.wait()

            if j == 1:
                project(0, both(step - 1))
                for s in both(step - 1):
                    unpack_rope(s)

        @pl.when(step == 1)
        def _():
            far_w.wait_recv()
            lax.fori_loop(1, chips, spread, 0)

        @pl.when(step == HALF_AT)
        def _():
            lax.fori_loop(1, chips, w_wait, 0)
            half_w.start()

        @pl.when(step >= Q1_FROM)
        def _():
            q_copy(1, nth(step - Q1_FROM)).start()

        @pl.when(step >= FAR_AT)
        def _():
            @pl.when(step == FAR_AT)
            def _():
                half_w.wait_recv()

            def unit(i, c):
                project(1, both((step - FAR_AT) * FAR_UNITS + i))
                return c

            lax.fori_loop(0, FAR_UNITS, unit, 0)

        return c

    lax.fori_loop(1, 7, ring_step, 0)
    for j in range(3):
        for way in (0, 1):
            ring_in(way, 6, subs[j], j).wait_recv()
        if j > 0:
            ring(j - 1, 7, halves[j - 1], 0).start()
    for i in range(7 - Q1_FROM, 6):
        q_copy(1, nth(i)).start()
    q_copy(1, q_farthest).start()

    def rest(i, c):
        project(lax.rem(i, 2), both(6 + i // 2))
        return c

    lax.fori_loop(0, 4, rest, 0)
    for i in (6, 7):
        for s in both(i):
            unpack_rope(s)
    for way in (0, 1):
        ring_in(way, 7, halves[way], 0).wait_recv()

    def last(shard, c):
        project(shard, (at(8),))
        return c

    lax.fori_loop(0, 2, last, 0)
    unpack_rope(at(8))

    factor = math.log2(math.e) / math.sqrt(QW)
    o_away = (1, -1, 2, -2, 3, -3, 8 * odd - 4)

    def o_place(shard, pair, slot):
        cols = shard_of(me, shard) * (HEADS_HERE * VDIM) + pair * (2 * VDIM)
        return (
            obuf.at[shard * 4 + pair, pl.ds(pl.multiple_of(slot * NEW, 16), NEW), :],
            out_hbm.at[:, pl.ds(pl.multiple_of(cols, 128), 2 * VDIM)],
        )

    def o_copy(shard, pair, d):
        src, dst = o_place(shard, pair, d - first_of(me))
        return pltpu.make_async_remote_copy(
            src, dst, o_s.at[shard, pair, lax.rem(d + SEQ, SEQ)], o_r.at[shard, pair, lax.rem(d + SEQ, SEQ)],
            device_id={"seq": at(d)}, device_id_type=MESH,
        )

    def o_own(shard, pair):
        src, dst = o_place(shard, pair, -first_of(me))
        return pltpu.make_async_copy(src, dst, loc_o.at[shard, pair])

    def attend(i, c):
        shard, pair = i // 4, lax.rem(i, 4)

        @pl.when(i == 0)
        def _():
            q_wait(0)

        @pl.when(i == 4)
        def _():
            q_wait(1)

        qp = qbuf[shard, :, pl.ds(pl.multiple_of(pair * (2 * QW), 128), 2 * QW)]
        qp = mm(qp, perm[...]).astype(BF)
        ss = []
        for n in range(2):
            head = shard * HEADS_HERE + 2 * pair + n
            keys = jnp.concatenate([kbuf[head], ropes[...]], axis=1)
            ss.append(mm_t(qp[:, 256 * n : 256 * n + 256], keys))
        for n in range(2):
            head = shard * HEADS_HERE + 2 * pair + n
            s = ss[n]
            s = jnp.concatenate([s[:, 0:PRE_ALL], s[:, PRE_ALL:] + bias[...]], axis=1)
            top = jnp.max(s, axis=1, keepdims=True)
            e = jnp.exp2((s - top) * factor)
            total = jnp.sum(e, axis=1, keepdims=True)
            o = mm(e.astype(BF), vbuf[head]) / total
            obuf[i, :, VDIM * n : VDIM * n + VDIM] = o.astype(BF)
        o_own(shard, pair).start()
        for d in o_away:
            o_copy(shard, pair, d).start()
        return c

    lax.fori_loop(0, 8, attend, 0)

    def o_wait(i, c):
        shard, pair = i // 4, lax.rem(i, 4)
        o_own(shard, pair).wait()
        for d in o_away:
            o_copy(shard, pair, d).wait_send()
            o_copy(shard, pair, d).wait_recv()
        return c

    lax.fori_loop(0, 8, o_wait, 0)
    for shard in (0, 1):
        for d in q_away:
            q_copy(shard, d).wait_send()
    far_w.wait_send()

    def w_sent(d, c):
        w_copy(d).wait_send()
        return c

    lax.fori_loop(1, chips, w_sent, 0)
    half_w.wait_send()

    def ring_sent(step, c):
        for way in (0, 1):
            for j in range(3):
                ring(way, step, subs[j], j).wait_send()
        return c

    lax.fori_loop(0, 7, ring_sent, 0)
    for way in (0, 1):
        ring(way, 7, halves[way], 0).wait_send()


def body(queries, stretch_latent, prefix_latent, kv_up_weight):
    reps = lax.axis_size("rep")
    dma = pltpu.SemaphoreType.DMA
    hbm = pl.BlockSpec(memory_space=pltpu.HBM)
    return pl.pallas_call(
        functools.partial(kernel, reps),
        out_shape=jax.ShapeDtypeStruct((NEW, SEQ * HEADS_HERE * VDIM), BF),
        in_specs=[hbm] * 4,
        out_specs=pl.BlockSpec(memory_space=pl.ANY),
        scratch_shapes=[
            pltpu.VMEM((PRE + NEW, KV_RANK + ROPE), BF),
            pltpu.VMEM((SEQ, CHUNK, KV_RANK), BF),
            pltpu.VMEM((2, ROWS, HEADS_HERE * QW), BF),
            pltpu.VMEM((2, KV_RANK, HEADS_HERE * SPAN), BF),
            pltpu.VMEM((2 * HEADS_HERE, KEYS, NOPE), BF),
            pltpu.VMEM((2 * HEADS_HERE, KEYS, VDIM), BF),
            pltpu.VMEM((KEYS, 128), BF),
            pltpu.VMEM((HEADS_HERE, ROWS, 2 * VDIM), BF),
            pltpu.VMEM((2 * QW, 512), BF),
            pltpu.VMEM((128, 256), BF),
            pltpu.VMEM((ROWS, SEQ * NEW), F32),
            dma((2, 8, 3)), dma((2, 8, 3)),
            dma((2, SEQ)), dma((2, SEQ)),
            dma((2, 4, SEQ)), dma((2, 4, SEQ)),
            dma, dma, dma((reps // 2,)), dma((reps // 2,)), dma, dma,
            dma, dma((2,)), dma((2,)), dma((2, 4)),
        ],
        compiler_params=pltpu.CompilerParams(
            collective_id=0, has_side_effects=True, vmem_limit_bytes=60 * 1024 * 1024
        ),
        cost_estimate=pl.CostEstimate(flops=13_000_000_000, bytes_accessed=8_000_000, transcendentals=4_200_000),
    )(prefix_latent, stretch_latent, queries, kv_up_weight)


def solution(mesh):
    in_specs = (
        P(("rep", "seq"), None),
        P(("rep", "seq"), None),
        P(("rep", "seq"), None),
        P(None, "seq"),
    )
    out_specs = P(("rep", "seq"), None)
    return jax.shard_map(body, mesh=mesh, in_specs=in_specs, out_specs=out_specs, check_vma=False)
```
